32 devices in a mesh: tm: 8 (over z, y), rep: 4 (over x, core).
Axes of the slice: x: 2, y: 2, z: 4, core: 2. Of those that a mesh axis runs over, the one named last changes fastest.
Arguments:
- separator_inverse: bfloat16 [32, 384, 384], P(('rep', 'tm')), parts along dimension 0, may hold values from -1 to 3, as said below
- separator_lower: bfloat16 [32, 384, 384], P(('rep', 'tm')), parts along dimension 0, may hold values from -0.15625 to 0.15625
- separator_upper: bfloat16 [32, 384, 384], P(('rep', 'tm')), parts along dimension 0, may hold values from -0.15625 to 0.15625
- top_diagonal: bfloat16 [32, 384, 384], P(('rep', 'tm')), parts along dimension 0, may hold values from -1 to 3, as said below
- top_coupling: bfloat16 [32, 384, 384], P(('rep', 'tm')), parts along dimension 0, may hold values from -0.3125 to 0.3125
- interior_inverse: bfloat16 [32, 384, 384], P(('rep', 'tm')), parts along dimension 0, may hold values from -1 to 3, as said below
- interior_lower: bfloat16 [32, 384, 384], P(('rep', 'tm')), parts along dimension 0, may hold values from -0.15625 to 0.15625
- interior_upper: bfloat16 [32, 384, 384], P(('rep', 'tm')), parts along dimension 0, may hold values from -0.15625 to 0.15625
Outputs:
- inverse_diagonal: bfloat16 [64, 384, 384], P(('rep', 'tm')), parts along dimension 0
- inverse_below: bfloat16 [64, 384, 384], P(('rep', 'tm')), parts along dimension 0
The draws below stay inside these ranges and needn't reach their ends.
There are 4 independent parts, one for each index of `rep`. The reference program is written for one: setup_inputs(seed, part) draws one part's arguments, and reference() takes and returns one part's arrays. A program takes and returns all parts, laid end to end along the dimension named above; each array names one. Nothing has to cross between parts.
Inputs may be any that keep to these rules, and one draw needn't show every extreme that they name: `separator_inverse`: every block is symmetric. `top_diagonal`: every block is symmetric. `interior_inverse`: every block is symmetric.
All inputs are finite; a program needn't handle non-finite values.
Results may differ from the reference program's by a relative error of at most 0.006.
Values may be sent and summed in bfloat16 or wider, within the bound.
A program may use at most 64 MiB of HBM per device.

```python
import math
import jax
import jax.numpy as jnp

B = 384
SEPS = 8
LEVELS = 2
TOPGAP = 4


def symmetric_blocks(key):
    diag_key, jitter_key = jax.random.split(key)
    diagonal = jnp.exp(jax.random.uniform(diag_key, (SEPS, B), jnp.float32, math.log(0.5), math.log(2.0)))
    jitter = jnp.clip(jax.random.normal(jitter_key, (SEPS, B, B), jnp.float32), -5.0, 5.0)
    jitter = jitter * (0.6 / math.sqrt(B))
    symmetric = (jitter + jnp.swapaxes(jitter, 1, 2)) * 0.7071
    identity = jnp.eye(B, dtype=jnp.float32)
    return (symmetric + diagonal[:, :, None] * identity[None, :, :]).astype(jnp.bfloat16)


def draw_separator_inverse(key, part):
    return symmetric_blocks(jax.random.fold_in(key, 11))


def draw_top_diagonal(key, part):
    return symmetric_blocks(jax.random.fold_in(key, 23))


def draw_interior_inverse(key, part):
    return symmetric_blocks(jax.random.fold_in(key, 37))


def levels(stream_key, extent, cuts, low, top_value):
    def one(axis_at, blocks):
        draws = jax.random.uniform(jax.random.fold_in(jax.random.fold_in(stream_key, 6), axis_at), (blocks,), jnp.float32, low / len(cuts), top_value / len(cuts))
        return jnp.repeat(jnp.exp(draws), extent[axis_at] // blocks).reshape((-1,) + (1,) * (len(extent) - axis_at - 1))

    gain = one(*cuts[0])
    for cut in cuts[1:]:
        gain = gain * one(*cut)
    return gain


def scatter_about(stream_key, shape, width, limit, cuts=(), kind=jnp.bfloat16):
    values = width * jax.random.normal(stream_key, shape, jnp.float32)
    if cuts:
        values = values * levels(stream_key, shape, cuts, -0.22, 0.18)
    return jnp.clip(values, -limit, limit).astype(kind)


def setup_inputs(seed: int = 0, part: int = 0) -> dict:
    splits = jax.random.split(jax.random.key(seed), 9)
    own_keys = jax.random.split(jax.random.fold_in(splits[8], part), 9)
    separator_inverse = draw_separator_inverse(jax.random.fold_in(jax.random.fold_in(splits[8], part), 71), part)
    separator_lower = scatter_about(own_keys[1], (SEPS, B, B), (4 * B) ** -0.5, 0.15625, ((0, 8),))
    separator_upper = scatter_about(own_keys[2], (SEPS, B, B), (4 * B) ** -0.5, 0.15625, ((0, 8),))
    top_diagonal = draw_top_diagonal(jax.random.fold_in(jax.random.fold_in(splits[8], part), 71), part)
    top_coupling = scatter_about(own_keys[4], (SEPS, B, B), B ** -0.5, 0.3125, ((0, 8),))
    interior_inverse = draw_interior_inverse(jax.random.fold_in(jax.random.fold_in(splits[8], part), 71), part)
    interior_lower = scatter_about(own_keys[6], (SEPS, B, B), (4 * B) ** -0.5, 0.15625, ((0, 8),))
    interior_upper = scatter_about(own_keys[7], (SEPS, B, B), (4 * B) ** -0.5, 0.15625, ((0, 8),))
    return dict(separator_inverse=separator_inverse, separator_lower=separator_lower, separator_upper=separator_upper, top_diagonal=top_diagonal, top_coupling=top_coupling, interior_inverse=interior_inverse, interior_lower=interior_lower, interior_upper=interior_upper)


def product(left_op, right_op):
    return jnp.einsum("nij,njk->nik", left_op.astype(jnp.float32), right_op.astype(jnp.float32))


def product_transposed(left_op, right_op):
    return jnp.einsum("nij,nkj->nik", left_op.astype(jnp.float32), right_op.astype(jnp.float32))


def descend(inverse, lower_mult, upper_mult, lower_diagonal, coupling, upper_diagonal):
    toward_lower = (product(lower_mult, lower_diagonal) + product(upper_mult, coupling)).astype(jnp.bfloat16)
    toward_upper = (product_transposed(lower_mult, coupling) + product(upper_mult, upper_diagonal)).astype(jnp.bfloat16)
    diagonal_new = (inverse.astype(jnp.float32) + product_transposed(toward_lower, lower_mult)
                    + product_transposed(toward_upper, upper_mult)).astype(jnp.bfloat16)
    return toward_lower, toward_upper, diagonal_new


def reference(separator_inverse, separator_lower, separator_upper, top_diagonal, top_coupling,
              interior_inverse, interior_lower, interior_upper):
    margin = TOPGAP // 2

    def rolled(field):
        return jnp.roll(field, margin, axis=0)

    def unrolled(field):
        return jnp.roll(field, -margin, axis=0)

    separator_inverse = rolled(separator_inverse)
    separator_lower = rolled(separator_lower)
    separator_upper = rolled(separator_upper)
    top_diagonal = rolled(top_diagonal)
    top_coupling = rolled(top_coupling)
    interior_inverse = rolled(interior_inverse)
    interior_lower = rolled(interior_lower)
    interior_upper = rolled(interior_upper)
    places = jnp.arange(SEPS)
    blank = jnp.zeros((SEPS, B, B), jnp.bfloat16)
    topmost = (places % TOPGAP == 0)
    sigma_diagonal = jnp.where(topmost[:, None, None], top_diagonal, blank)
    sigma_upper = jnp.where(topmost[:, None, None], top_coupling, blank)
    sigma_lower = blank
    for height in range(LEVELS, 0, -1):
        offset = 2 ** (height - 1)
        stride = 2 * offset
        lower_diagonal = sigma_diagonal[0::stride]
        lower_coupling = sigma_upper[0::stride]
        upper_diagonal = jnp.roll(sigma_diagonal[0::stride], -1, axis=0)
        upper_coupling = jnp.roll(sigma_lower[0::stride], -1, axis=0)
        members = lower_diagonal.shape[0]
        lower_holds = (jnp.arange(members) % 2 == 1) | (height == LEVELS)
        coupling = jnp.where(lower_holds[:, None, None], jnp.swapaxes(lower_coupling, 1, 2), upper_coupling)
        toward_lower, toward_upper, diagonal_new = descend(
            separator_inverse[offset::stride], separator_lower[offset::stride], separator_upper[offset::stride],
            lower_diagonal, coupling, upper_diagonal)
        sigma_lower = sigma_lower.at[offset::stride].set(toward_lower)
        sigma_upper = sigma_upper.at[offset::stride].set(toward_upper)
        sigma_diagonal = sigma_diagonal.at[offset::stride].set(diagonal_new)
    next_diagonal = jnp.roll(sigma_diagonal, -1, axis=0)
    next_lower = jnp.roll(sigma_lower, -1, axis=0)
    odd_slab = (places % 2 == 1)
    coupling = jnp.where(odd_slab[:, None, None], jnp.swapaxes(sigma_upper, 1, 2), next_lower)
    below_own, below_next, interior_diagonal = descend(
        interior_inverse, interior_lower, interior_upper, sigma_diagonal, coupling, next_diagonal)
    sigma_diagonal = unrolled(sigma_diagonal)
    interior_diagonal = unrolled(interior_diagonal)
    below_own = unrolled(below_own)
    below_next = unrolled(below_next)
    inverse_diagonal = jnp.stack([sigma_diagonal, interior_diagonal], axis=1).reshape(2 * SEPS, B, B)
    inverse_below = jnp.stack([below_own, jnp.swapaxes(below_next, 1, 2)], axis=1).reshape(2 * SEPS, B, B)
    return inverse_diagonal, inverse_below
```

```python
import functools

import jax
import jax.numpy as jnp
from jax import lax
from jax.experimental import pallas as pl
from jax.experimental.pallas import tpu as pltpu
from jax.sharding import PartitionSpec as P

MESH = pl.DeviceIdType.MESH
TILE = 128


def product(left_op, right_op):
    return jnp.dot(left_op, right_op, preferred_element_type=jnp.float32)


def product_transposed(left_op, right_op):
    return lax.dot_general(
        left_op, right_op, (((1,), (1,)), ((), ())), preferred_element_type=jnp.float32
    )


def strips(size):
    tile = TILE if size % TILE == 0 else size
    return [(at, tile) for at in range(0, size, tile)]


def strip(ref, at, rows):
    size = ref.shape[-1]
    return ref.at[pl.ds(at, rows), pl.ds(at, size - at)]


def mirror(ref):
    for at, rows in strips(ref.shape[-1]):
        for other, others in strips(ref.shape[-1]):
            if other > at:
                ref[pl.ds(other, others), pl.ds(at, rows)] = ref[
                    pl.ds(at, rows), pl.ds(other, others)
                ].T


class Mail:
    def __init__(self, dst, send_sem, send_at, recv_sem, recv_at, symmetric):
        self.dst, self.symmetric = dst, symmetric
        self.send_sem, self.send_at = send_sem, send_at
        self.recv_sem, self.recv_at = recv_sem, recv_at
        self.pieces = strips(dst.shape[-1]) if symmetric else [None]

    def copy(self, src, to, piece):
        dst = self.dst
        if self.symmetric:
            src, dst = strip(src, *self.pieces[piece]), strip(dst, *self.pieces[piece])
        return pltpu.make_async_remote_copy(
            src_ref=src,
            dst_ref=dst,
            send_sem=self.send_sem.at[self.send_at + piece],
            recv_sem=self.recv_sem.at[self.recv_at + piece],
            device_id={"tm": to},
            device_id_type=MESH,
        )

    def start(self, src, to):
        for piece in range(len(self.pieces)):
            self.copy(src, to, piece).start()

    def wait_send(self, src, to):
        for piece in range(len(self.pieces)):
            self.copy(src, to, piece).wait_send()

    def wait_recv(self, to):
        for piece in range(len(self.pieces)):
            self.copy(self.dst, to, piece).wait_recv()

    def relay(self, incoming, to):
        for piece in range(len(self.pieces)):
            incoming.copy(incoming.dst, to, piece).wait_recv()
            self.copy(incoming.dst, to, piece).start()


def semaphore_counts(levels, pieces):
    per_level = 2 * pieces + 2
    sends = (levels - 1) * per_level + (1 + pieces) + (1 + 2 * pieces) + (2 + pieces)
    receives = (1 + 2 * pieces) + (3 + 3 * pieces)
    return sends, receives


def kernel(
    devices,
    levels,
    sep_inv,
    sep_lower,
    sep_upper,
    top_diag,
    top_coup,
    int_inv,
    int_lower,
    int_upper,
    out_diag,
    out_below,
    inv,
    low,
    upp,
    diag,
    up,
    down,
    diag_a,
    diag_b,
    coup,
    inv1,
    low1,
    upp1,
    diag_a1,
    diag_b1,
    coup1,
    up1,
    down1,
    diag1,
    iinv,
    ilow,
    iupp,
    idiag,
    below,
    below_t,
    send_sem,
    recv_sem,
    load_sem,
    store_sem,
):
    size = sep_inv.shape[-1]
    pieces = len(strips(size))
    spacing = 2**levels
    me = lax.axis_index("tm")
    position = lax.rem(me + spacing // 2, devices)
    odd = lax.rem(position, 2) == 1
    even = lax.rem(position, 2) == 0
    top = lax.rem(position, spacing) == 0

    def near(steps):
        return lax.rem(me + steps + devices, devices)

    def load(src, dst, at):
        return pltpu.make_async_copy(src.at[0], dst, load_sem.at[at])

    def store(src, dst, at):
        return pltpu.make_async_copy(src, dst, store_sem.at[at])

    counts = {"send": 0, "recv": 0}

    def take(kind, number):
        counts[kind] += number
        return counts[kind] - number

    def receives(symmetric):
        return take("recv", pieces if symmetric else 1)

    def mail(dst, recv_at, symmetric):
        send_at = take("send", pieces if symmetric else 1)
        return Mail(dst, send_sem, send_at, recv_sem, recv_at, symmetric)

    at_a, at_b, at_c = receives(True), receives(True), receives(False)
    at_a1, at_b1, at_c1 = receives(True), receives(True), receives(False)
    at_inv1, at_low1, at_upp1 = receives(True), receives(False), receives(False)
    level_mail = {}
    for height in range(levels, 1, -1):
        level_mail[height] = dict(
            a=mail(diag_a, at_a, True),
            b=mail(diag_b, at_b, True),
            c_up=mail(coup, at_c, False),
            c_down=mail(coup, at_c, False),
        )
    feed_c, feed_b = mail(coup1, at_c1, False), mail(diag_b1, at_b1, True)
    odd_a, odd_b, odd_c = mail(diag_a1, at_a1, True), mail(diag_b1, at_b1, True), mail(coup1, at_c1, False)
    back_inv, back_low, back_upp = (
        mail(inv1, at_inv1, True),
        mail(low1, at_low1, False),
        mail(upp1, at_upp1, False),
    )

    @pl.when(even)
    def _():
        load(sep_lower, low, 0).start()
        load(sep_upper, upp, 1).start()
        load(sep_inv, inv, 2).start()

    @pl.when(odd)
    def _():
        load(sep_lower, low1, 0).start()
        load(sep_upper, upp1, 1).start()
        load(sep_inv, inv1, 2).start()

    @pl.when(top)
    def _():
        load(top_diag, diag, 3).start()

    load(int_lower, ilow, 5).start()
    load(int_upper, iupp, 6).start()
    load(int_inv, iinv, 7).start()

    barrier = pltpu.get_barrier_semaphore()
    reach = [sign * 2**power for power in range(levels) for sign in (1, -1)]
    for steps in reach:
        pl.semaphore_signal(barrier, inc=1, device_id={"tm": near(steps)}, device_id_type=MESH)
    pl.semaphore_wait(barrier, len(reach))

    def holds(height):
        return lax.rem(position, 2**height) == 0

    def coupled(height):
        return lax.rem(position // 2**height, 2) == 1

    def sends(height, act):
        offset = 2 ** (height - 1)
        mails = level_mail[height]
        if height == levels:
            diag_src, up_src = top_diag.at[0], top_coup.at[0]
        else:
            diag_src, up_src = diag, up

        def act_up():
            act(mails["c_up"], up_src, near(offset))

        def act_down():
            act(mails["c_down"], down, near(-offset))

        if height == levels:
            act_up()
        else:
            pl.when(coupled(height))(act_up)
            pl.when(coupled(height))(act_down)
        act(mails["b"], diag_src, near(-offset))
        act(mails["a"], diag_src, near(offset))

    def start(message, src, to):
        message.start(src, to)

    def finish(message, src, to):
        message.wait_send(src, to)

    pl.when(holds(levels))(lambda: sends(levels, start))

    @pl.when(odd)
    def _():
        back_low.start(sep_lower.at[0], near(-1))
        back_upp.start(sep_upper.at[0], near(-1))
        back_inv.start(sep_inv.at[0], near(-1))

    @pl.when(even)
    def _():
        load(sep_lower, low, 0).wait()
        load(sep_upper, upp, 1).wait()
        load(sep_inv, inv, 2).wait()

    @pl.when(top)
    def _():
        load(top_diag, diag, 3).wait()

    parent = lax.rem(position, 4) == 2
    other = lax.rem(position, 4) == 0

    for height in range(levels, 1, -1):
        offset = 2 ** (height - 1)
        mails = level_mail[height]
        if height < levels:
            pl.when(holds(height))(functools.partial(sends, height, start))

        @pl.when(lax.rem(position, 2**height) == offset)
        def _():
            mails["c_up"].wait_recv(me)
            if height == levels:
                flipped = coup[...].T
            else:
                from_below = jnp.where(coupled(height), 1.0, 0.0)
                value = coup[...].astype(jnp.float32)
                flipped = jnp.where(from_below > 0.5, value.T, value).astype(jnp.bfloat16)
            if height == 2:
                mails["b"].wait_recv(me)
                mirror(diag_b)
                odd_b.start(diag_b, near(1))
            else:
                mails["b"].wait_recv(me)
                mirror(diag_b)
            toward_upper = product_transposed(low[...], flipped) + product(upp[...], diag_b[...])
            up[...] = toward_upper.astype(jnp.bfloat16)
            if height == 2:
                coup1[...] = up[...].T
                odd_c.start(coup1, near(1))
            mails["a"].wait_recv(me)
            mirror(diag_a)
            toward_lower = product(low[...], diag_a[...]) + product(upp[...], flipped)
            down[...] = toward_lower.astype(jnp.bfloat16)
            if height == 2:
                feed_c.start(down, near(-2))
            diagonal = (
                inv[...].astype(jnp.float32)
                + product_transposed(down[...], low[...])
                + product_transposed(up[...], upp[...])
            )
            diag[...] = diagonal.astype(jnp.bfloat16)
            if height == 2:
                feed_b.start(diag, near(-2))
                diag_b1[...] = diag_b[...]

    @pl.when(even)
    def _():
        odd_a.start(diag, near(1))
        store(diag, out_diag.at[0], 0).start()
        diag_a1[...] = diag[...]
        back_low.wait_recv(me)
        back_upp.wait_recv(me)

    @pl.when(other)
    def _():
        odd_c.relay(feed_c, near(1))
        odd_b.relay(feed_b, near(1))
        mirror(diag_b1)

    @pl.when(odd)
    def _():
        load(sep_lower, low1, 0).wait()
        load(sep_upper, upp1, 1).wait()
        load(sep_inv, inv1, 2).wait()
        odd_b.wait_recv(me)
        mirror(diag_b1)
        odd_c.wait_recv(me)

    toward_upper = product_transposed(low1[...], coup1[...]) + product(upp1[...], diag_b1[...])
    up1[...] = toward_upper.astype(jnp.bfloat16)

    @pl.when(odd)
    def _():
        odd_a.wait_recv(me)
        mirror(diag_a1)

    toward_lower = product(low1[...], diag_a1[...]) + product(upp1[...], coup1[...])
    down1[...] = toward_lower.astype(jnp.bfloat16)

    @pl.when(even)
    def _():
        back_inv.wait_recv(me)
        mirror(inv1)

    diagonal = (
        inv1[...].astype(jnp.float32)
        + product_transposed(down1[...], low1[...])
        + product_transposed(up1[...], upp1[...])
    )
    diag1[...] = diagonal.astype(jnp.bfloat16)

    load(int_lower, ilow, 5).wait()
    load(int_upper, iupp, 6).wait()
    load(int_inv, iinv, 7).wait()

    def interior(own, coupling, following):
        own_value = (product(ilow[...], own[...]) + product(iupp[...], coupling)).astype(
            jnp.bfloat16
        )
        below[...] = own_value
        store(below, out_below.at[0], 1).start()
        next_value = (
            product_transposed(ilow[...], coupling) + product(iupp[...], following[...])
        ).astype(jnp.bfloat16)
        below_t[...] = next_value.T
        store(below_t, out_below.at[1], 2).start()
        diagonal = (
            iinv[...].astype(jnp.float32)
            + product_transposed(own_value, ilow[...])
            + product_transposed(next_value, iupp[...])
        )
        idiag[...] = diagonal.astype(jnp.bfloat16)
        store(idiag, out_diag.at[1], 3).start()

    @pl.when(odd)
    def _():
        store(diag1, out_diag.at[0], 0).start()
        interior(diag1, up1[...].T, diag_b1)

    @pl.when(even)
    def _():
        interior(diag_a1, down1[...], diag1)

    for height in range(levels, 1, -1):
        pl.when(holds(height))(functools.partial(sends, height, finish))

    @pl.when(parent)
    def _():
        feed_c.wait_send(down, near(-2))
        feed_b.wait_send(diag, near(-2))

    @pl.when(even)
    def _():
        odd_a.wait_send(diag, near(1))
        odd_b.wait_send(diag_b1, near(1))
        odd_c.wait_send(coup1, near(1))

    @pl.when(odd)
    def _():
        back_low.wait_send(sep_lower.at[0], near(-1))
        back_upp.wait_send(sep_upper.at[0], near(-1))
        back_inv.wait_send(sep_inv.at[0], near(-1))

    store(diag, out_diag.at[0], 0).wait()
    store(below, out_below.at[0], 1).wait()
    store(below_t, out_below.at[1], 2).wait()
    store(idiag, out_diag.at[1], 3).wait()


def solution(mesh):
    devices = mesh.shape["tm"]
    levels = min(4, devices // 4)

    def on_device(*blocks):
        size = blocks[0].shape[-1]
        sends, receives = semaphore_counts(levels, len(strips(size)))
        block = pltpu.VMEM((size, size), jnp.bfloat16)
        out = jax.ShapeDtypeStruct((2, size, size), jnp.bfloat16)
        return pl.pallas_call(
            functools.partial(kernel, devices, levels),
            out_shape=(out, out),
            in_specs=[pl.BlockSpec(memory_space=pl.ANY)] * len(blocks),
            out_specs=[pl.BlockSpec(memory_space=pl.ANY)] * 2,
            scratch_shapes=[block] * 24
            + [
                pltpu.SemaphoreType.DMA((sends,)),
                pltpu.SemaphoreType.DMA((receives,)),
                pltpu.SemaphoreType.DMA((8,)),
                pltpu.SemaphoreType.DMA((4,)),
            ],
            compiler_params=pltpu.CompilerParams(
                collective_id=0, has_side_effects=True, vmem_limit_bytes=40 * 2**20
            ),
            cost_estimate=pl.CostEstimate(
                flops=36 * size**3, bytes_accessed=24 * size**2, transcendentals=0
            ),
        )(*blocks)

    spec = P(("rep", "tm"), None, None)
    return jax.shard_map(
        on_device, mesh=mesh, in_specs=(spec,) * 8, out_specs=(spec, spec), check_vma=False
    )
```

```python
import functools

import jax
import jax.numpy as jnp
from jax import lax
from jax.experimental import pallas as pl
from jax.experimental.pallas import tpu as pltpu
from jax.sharding import PartitionSpec as P

MESH = pl.DeviceIdType.MESH
TILE = 128


def product(left_op, right_op):
    return jnp.dot(left_op, right_op, preferred_element_type=jnp.float32)


def product_transposed(left_op, right_op):
    return lax.dot_general(
        left_op, right_op, (((1,), (1,)), ((), ())), preferred_element_type=jnp.float32
    )


def strips(size):
    tile = TILE if size % TILE == 0 else size
    return [(at, tile) for at in range(0, size, tile)]


def strip(ref, at, rows, symmetric):
    size = ref.shape[-1]
    first = at if symmetric else 0
    return ref.at[pl.ds(at, rows), pl.ds(first, size - first)]


def mirror(ref):
    for at, rows in strips(ref.shape[-1]):
        for other, others in strips(ref.shape[-1]):
            if other > at:
                ref[pl.ds(other, others), pl.ds(at, rows)] = ref[
                    pl.ds(at, rows), pl.ds(other, others)
                ].T


class Mail:
    def __init__(self, dst, send_sem, send_at, recv_sem, recv_at, symmetric):
        self.dst, self.symmetric = dst, symmetric
        self.send_sem, self.send_at = send_sem, send_at
        self.recv_sem, self.recv_at = recv_sem, recv_at
        self.pieces = strips(dst.shape[-1])

    def copy(self, src, to, piece):
        part = (*self.pieces[piece], self.symmetric)
        return pltpu.make_async_remote_copy(
            src_ref=strip(src, *part),
            dst_ref=strip(self.dst, *part),
            send_sem=self.send_sem.at[self.send_at + piece],
            recv_sem=self.recv_sem.at[self.recv_at + piece],
            device_id={"tm": to},
            device_id_type=MESH,
        )

    def start(self, src, to):
        for piece in range(len(self.pieces)):
            self.copy(src, to, piece).start()

    def wait_send(self, src, to):
        for piece in range(len(self.pieces)):
            self.copy(src, to, piece).wait_send()

    def wait_recv(self, to):
        for piece in range(len(self.pieces)):
            self.copy(self.dst, to, piece).wait_recv()

    def relay(self, incoming, to):
        for piece in range(len(self.pieces)):
            incoming.copy(incoming.dst, to, piece).wait_recv()
            self.copy(incoming.dst, to, piece).start()


def semaphore_counts(levels, pieces):
    return (4 * (levels - 1) + 10) * pieces, 9 * pieces


def kernel(
    devices,
    levels,
    sep_inv,
    sep_lower,
    sep_upper,
    top_diag,
    top_coup,
    int_inv,
    int_lower,
    int_upper,
    out_diag,
    out_below,
    inv,
    low,
    upp,
    diag,
    up,
    down,
    diag_a,
    diag_b,
    coup,
    inv1,
    low1,
    upp1,
    diag_a1,
    diag_b1,
    coup1,
    up1,
    down1,
    diag1,
    iinv,
    ilow,
    iupp,
    idiag,
    below,
    below_t,
    send_sem,
    recv_sem,
    load_sem,
    store_sem,
):
    size = sep_inv.shape[-1]
    pieces = len(strips(size))
    spacing = 2**levels
    me = lax.axis_index("tm")
    position = lax.rem(me + spacing // 2, devices)
    odd = lax.rem(position, 2) == 1
    even = lax.rem(position, 2) == 0
    top = lax.rem(position, spacing) == 0

    def near(steps):
        return lax.rem(me + steps + devices, devices)

    def load(src, dst, at):
        return pltpu.make_async_copy(src.at[0], dst, load_sem.at[at])

    def store(src, dst, at):
        return pltpu.make_async_copy(src, dst, store_sem.at[at])

    counts = {"send": 0, "recv": 0}

    def take(kind, number):
        counts[kind] += number
        return counts[kind] - number

    def receives(symmetric):
        return take("recv", pieces)

    def mail(dst, recv_at, symmetric):
        send_at = take("send", pieces)
        return Mail(dst, send_sem, send_at, recv_sem, recv_at, symmetric)

    at_a, at_b, at_c = receives(True), receives(True), receives(False)
    at_a1, at_b1, at_c1 = receives(True), receives(True), receives(False)
    at_inv1, at_low1, at_upp1 = receives(True), receives(False), receives(False)
    level_mail = {}
    for height in range(levels, 1, -1):
        level_mail[height] = dict(
            a=mail(diag_a, at_a, True),
            b=mail(diag_b, at_b, True),
            c_up=mail(coup, at_c, False),
            c_down=mail(coup, at_c, False),
        )
    feed_c, feed_b = mail(coup1, at_c1, False), mail(diag_b1, at_b1, True)
    odd_a, odd_b, odd_c = (
        mail(diag_a1, at_a1, True),
        mail(diag_b1, at_b1, True),
        mail(coup1, at_c1, False),
    )
    rail_b, even_b = mail(diag_b1, at_b1, True), mail(diag_b1, at_b1, True)
    back_inv, back_low, back_upp = (
        mail(inv1, at_inv1, True),
        mail(low1, at_low1, False),
        mail(upp1, at_upp1, False),
    )

    @pl.when(even)
    def _():
        load(sep_lower, low, 0).start()
        load(sep_upper, upp, 1).start()
        load(sep_inv, inv, 2).start()

    @pl.when(odd)
    def _():
        load(sep_lower, low1, 0).start()
        load(sep_upper, upp1, 1).start()
        load(sep_inv, inv1, 2).start()

    @pl.when(top)
    def _():
        load(top_diag, diag, 3).start()

    load(int_lower, ilow, 5).start()
    load(int_upper, iupp, 6).start()
    load(int_inv, iinv, 7).start()

    barrier = pltpu.get_barrier_semaphore()
    reach = [sign * 2**power for power in range(levels) for sign in (1, -1)]
    for steps in reach:
        pl.semaphore_signal(barrier, inc=1, device_id={"tm": near(steps)}, device_id_type=MESH)
    pl.semaphore_wait(barrier, len(reach))

    def holds(height):
        return lax.rem(position, 2**height) == 0

    def coupled(height):
        return lax.rem(position // 2**height, 2) == 1

    def sends(height, act):
        offset = 2 ** (height - 1)
        mails = level_mail[height]
        if height == levels:
            diag_src, up_src = top_diag.at[0], top_coup.at[0]
        else:
            diag_src, up_src = diag, up

        def act_up():
            act(mails["c_up"], up_src, near(offset))

        def act_down():
            act(mails["c_down"], down, near(-offset))

        if height == levels:
            act_up()
        else:
            pl.when(coupled(height))(act_up)
            pl.when(coupled(height))(act_down)
        act(mails["a"], diag_src, near(offset))
        if height > 2:
            act(mails["b"], diag_src, near(-offset))

    def start(message, src, to):
        message.start(src, to)

    def finish(message, src, to):
        message.wait_send(src, to)

    parent = lax.rem(position, 4) == 2
    other = lax.rem(position, 4) == 0
    first_odd = lax.rem(position, 4) == 1
    last_odd = lax.rem(position, 4) == 3

    @pl.when(top)
    def _():
        odd_a.start(top_diag.at[0], near(1))
        sends(levels, start)

    @pl.when(odd)
    def _():
        back_low.start(sep_lower.at[0], near(-1))

    @pl.when(first_odd)
    def _():
        back_upp.start(sep_upper.at[0], near(-1))
        back_inv.start(sep_inv.at[0], near(-1))
        rail_b.relay(odd_a, near(-2))
        mirror(diag_a1)

    @pl.when(last_odd)
    def _():
        even_b.relay(rail_b, near(-1))
        back_upp.start(sep_upper.at[0], near(-1))
        back_inv.start(sep_inv.at[0], near(-1))
        mirror(diag_b1)

    @pl.when(even)
    def _():
        load(sep_lower, low, 0).wait()
        load(sep_upper, upp, 1).wait()
        load(sep_inv, inv, 2).wait()

    @pl.when(top)
    def _():
        load(top_diag, diag, 3).wait()

    for height in range(levels, 1, -1):
        offset = 2 ** (height - 1)
        mails = level_mail[height]
        if height < levels:
            pl.when(holds(height))(functools.partial(sends, height, start))

        @pl.when(lax.rem(position, 2**height) == offset)
        def _():
            mails["c_up"].wait_recv(me)
            if height == levels:
                flipped = coup[...].T
            else:
                from_below = jnp.where(coupled(height), 1.0, 0.0)
                value = coup[...].astype(jnp.float32)
                flipped = jnp.where(from_below > 0.5, value.T, value).astype(jnp.bfloat16)
            if height == 2:
                even_b.wait_recv(me)
                upper = diag_b1
            else:
                mails["b"].wait_recv(me)
                upper = diag_b
            mirror(upper)
            toward_upper = product_transposed(low[...], flipped) + product(upp[...], upper[...])
            up[...] = toward_upper.astype(jnp.bfloat16)
            if height == 2:
                coup1[...] = up[...].T
                odd_c.start(coup1, near(1))
            mails["a"].wait_recv(me)
            mirror(diag_a)
            toward_lower = product(low[...], diag_a[...]) + product(upp[...], flipped)
            down[...] = toward_lower.astype(jnp.bfloat16)
            if height == 2:
                feed_c.start(down, near(-2))
            diagonal = (
                inv[...].astype(jnp.float32)
                + product_transposed(down[...], low[...])
                + product_transposed(up[...], upp[...])
            )
            diag[...] = diagonal.astype(jnp.bfloat16)
            odd_a.start(diag, near(1))
            if height == 2:
                feed_b.start(diag, near(-2))

    @pl.when(even)
    def _():
        store(diag, out_diag.at[0], 0).start()
        diag_a1[...] = diag[...]
        back_low.wait_recv(me)
        back_upp.wait_recv(me)

    @pl.when(other)
    def _():
        odd_c.relay(feed_c, near(1))
        odd_b.relay(feed_b, near(1))
        mirror(diag_b1)

    @pl.when(odd)
    def _():
        load(sep_lower, low1, 0).wait()
        load(sep_upper, upp1, 1).wait()
        load(sep_inv, inv1, 2).wait()
        odd_c.wait_recv(me)

    @pl.when(first_odd)
    def _():
        odd_b.wait_recv(me)
        mirror(diag_b1)

    toward_upper = product_transposed(low1[...], coup1[...]) + product(upp1[...], diag_b1[...])
    up1[...] = toward_upper.astype(jnp.bfloat16)

    @pl.when(last_odd)
    def _():
        odd_a.wait_recv(me)
        mirror(diag_a1)

    toward_lower = product(low1[...], diag_a1[...]) + product(upp1[...], coup1[...])
    down1[...] = toward_lower.astype(jnp.bfloat16)

    @pl.when(even)
    def _():
        back_inv.wait_recv(me)
        mirror(inv1)

    diagonal = (
        inv1[...].astype(jnp.float32)
        + product_transposed(down1[...], low1[...])
        + product_transposed(up1[...], upp1[...])
    )
    diag1[...] = diagonal.astype(jnp.bfloat16)

    load(int_lower, ilow, 5).wait()
    load(int_upper, iupp, 6).wait()
    load(int_inv, iinv, 7).wait()

    def interior(own, coupling, following):
        own_value = (product(ilow[...], own[...]) + product(iupp[...], coupling)).astype(
            jnp.bfloat16
        )
        below[...] = own_value
        store(below, out_below.at[0], 1).start()
        next_value = (
            product_transposed(ilow[...], coupling) + product(iupp[...], following[...])
        ).astype(jnp.bfloat16)
        below_t[...] = next_value.T
        store(below_t, out_below.at[1], 2).start()
        diagonal = (
            iinv[...].astype(jnp.float32)
            + product_transposed(own_value, ilow[...])
            + product_transposed(next_value, iupp[...])
        )
        idiag[...] = diagonal.astype(jnp.bfloat16)
        store(idiag, out_diag.at[1], 3).start()

    @pl.when(odd)
    def _():
        store(diag1, out_diag.at[0], 0).start()
        interior(diag1, up1[...].T, diag_b1)

    @pl.when(even)
    def _():
        interior(diag_a1, down1[...], diag1)

    for height in range(levels, 1, -1):
        pl.when(holds(height))(functools.partial(sends, height, finish))

    @pl.when(parent)
    def _():
        feed_c.wait_send(down, near(-2))
        feed_b.wait_send(diag, near(-2))

    @pl.when(even)
    def _():
        odd_a.wait_send(diag, near(1))
        odd_c.wait_send(coup1, near(1))

    @pl.when(other)
    def _():
        odd_b.wait_send(diag_b1, near(1))

    @pl.when(first_odd)
    def _():
        rail_b.wait_send(diag_a1, near(-2))

    @pl.when(last_odd)
    def _():
        even_b.wait_send(diag_b1, near(-1))

    @pl.when(odd)
    def _():
        back_low.wait_send(sep_lower.at[0], near(-1))
        back_upp.wait_send(sep_upper.at[0], near(-1))
        back_inv.wait_send(sep_inv.at[0], near(-1))

    store(diag, out_diag.at[0], 0).wait()
    store(below, out_below.at[0], 1).wait()
    store(below_t, out_below.at[1], 2).wait()
    store(idiag, out_diag.at[1], 3).wait()


def solution(mesh):
    devices = mesh.shape["tm"]
    levels = min(4, devices // 4)

    def on_device(*blocks):
        size = blocks[0].shape[-1]
        sends, receives = semaphore_counts(levels, len(strips(size)))
        block = pltpu.VMEM((size, size), jnp.bfloat16)
        out = jax.ShapeDtypeStruct((2, size, size), jnp.bfloat16)
        return pl.pallas_call(
            functools.partial(kernel, devices, levels),
            out_shape=(out, out),
            in_specs=[pl.BlockSpec(memory_space=pltpu.HBM)] * len(blocks),
            out_specs=[pl.BlockSpec(memory_space=pltpu.HBM)] * 2,
            scratch_shapes=[block] * 24
            + [
                pltpu.SemaphoreType.DMA((sends,)),
                pltpu.SemaphoreType.DMA((receives,)),
                pltpu.SemaphoreType.DMA((8,)),
                pltpu.SemaphoreType.DMA((4,)),
            ],
            compiler_params=pltpu.CompilerParams(
                collective_id=0, has_side_effects=True, vmem_limit_bytes=63 * 2**20
            ),
            cost_estimate=pl.CostEstimate(
                flops=36 * size**3, bytes_accessed=24 * size**2, transcendentals=0
            ),
        )(*blocks)

    spec = P(("rep", "tm"), None, None)
    return jax.shard_map(
        on_device, mesh=mesh, in_specs=(spec,) * 8, out_specs=(spec, spec), check_vma=False
    )
```

```python
import functools

import jax
import jax.numpy as jnp
from jax import lax
from jax.experimental import pallas as pl
from jax.experimental.pallas import tpu as pltpu
from jax.sharding import PartitionSpec as P

MESH = pl.DeviceIdType.MESH
TILE = 128


def product(left_op, right_op):
    return jnp.dot(left_op, right_op, preferred_element_type=jnp.float32)


def product_transposed(left_op, right_op):
    return lax.dot_general(
        left_op, right_op, (((1,), (1,)), ((), ())), preferred_element_type=jnp.float32
    )


def strips(size):
    tile = TILE if size % TILE == 0 else size
    return [(at, tile) for at in range(0, size, tile)]


def strip(ref, at, rows, symmetric):
    size = ref.shape[-1]
    first = at if symmetric else 0
    return ref.at[pl.ds(at, rows), pl.ds(first, size - first)]


def mirror(ref):
    for at, rows in strips(ref.shape[-1]):
        for other, others in strips(ref.shape[-1]):
            if other > at:
                ref[pl.ds(other, others), pl.ds(at, rows)] = ref[
                    pl.ds(at, rows), pl.ds(other, others)
                ].T


class Mail:
    def __init__(self, dst, send_sem, send_at, recv_sem, recv_at, symmetric):
        self.dst, self.symmetric = dst, symmetric
        self.send_sem, self.send_at = send_sem, send_at
        self.recv_sem, self.recv_at = recv_sem, recv_at
        self.pieces = strips(dst.shape[-1])

    def copy(self, src, to, piece):
        part = (*self.pieces[piece], self.symmetric)
        return pltpu.make_async_remote_copy(
            src_ref=strip(src, *part),
            dst_ref=strip(self.dst, *part),
            send_sem=self.send_sem.at[self.send_at + piece],
            recv_sem=self.recv_sem.at[self.recv_at + piece],
            device_id={"tm": to},
            device_id_type=MESH,
        )

    def start(self, src, to):
        for piece in range(len(self.pieces)):
            self.copy(src, to, piece).start()

    def wait_send(self, src, to):
        for piece in range(len(self.pieces)):
            self.copy(src, to, piece).wait_send()

    def wait_recv(self, to):
        for piece in range(len(self.pieces)):
            self.copy(self.dst, to, piece).wait_recv()

    def relay(self, incoming, to):
        for piece in range(len(self.pieces)):
            incoming.copy(incoming.dst, to, piece).wait_recv()
            self.copy(incoming.dst, to, piece).start()


def semaphore_counts(levels, pieces):
    return (4 * (levels - 1) + 10) * pieces, 9 * pieces


def kernel(
    devices,
    levels,
    sep_inv,
    sep_lower,
    sep_upper,
    top_diag,
    top_coup,
    int_inv,
    int_lower,
    int_upper,
    out_diag,
    out_below,
    inv,
    low,
    upp,
    diag,
    up,
    down,
    diag_a,
    diag_b,
    coup,
    inv1,
    low1,
    upp1,
    diag_a1,
    diag_b1,
    coup1,
    up1,
    down1,
    diag1,
    iinv,
    ilow,
    iupp,
    part_side,
    part_diag,
    part_int,
    send_sem,
    recv_sem,
    load_sem,
):
    size = sep_inv.shape[-1]
    pieces = len(strips(size))
    spacing = 2**levels
    me = lax.axis_index("tm")
    position = lax.rem(me + spacing // 2, devices)
    odd = lax.rem(position, 2) == 1
    even = lax.rem(position, 2) == 0
    top = lax.rem(position, spacing) == 0

    def near(steps):
        return lax.rem(me + steps + devices, devices)

    def load(src, dst, at):
        return pltpu.make_async_copy(src.at[0], dst, load_sem.at[at])

    counts = {"send": 0, "recv": 0}

    def take(kind, number):
        counts[kind] += number
        return counts[kind] - number

    def receives(symmetric):
        return take("recv", pieces)

    def mail(dst, recv_at, symmetric):
        send_at = take("send", pieces)
        return Mail(dst, send_sem, send_at, recv_sem, recv_at, symmetric)

    at_a, at_b, at_c = receives(True), receives(True), receives(False)
    at_a1, at_b1, at_c1 = receives(True), receives(True), receives(False)
    at_inv1, at_low1, at_upp1 = receives(True), receives(False), receives(False)
    level_mail = {}
    for height in range(levels, 1, -1):
        level_mail[height] = dict(
            a=mail(diag_a, at_a, True),
            b=mail(diag_b, at_b, True),
            c_up=mail(coup, at_c, False),
            c_down=mail(coup, at_c, False),
        )
    feed_c, feed_b = mail(coup1, at_c1, False), mail(diag_b1, at_b1, True)
    odd_a, odd_b, odd_c = (
        mail(diag_a1, at_a1, True),
        mail(diag_b1, at_b1, True),
        mail(coup1, at_c1, False),
    )
    rail_b, even_b = mail(diag_b1, at_b1, True), mail(diag_b1, at_b1, True)
    back_inv, back_low, back_upp = (
        mail(inv1, at_inv1, True),
        mail(low1, at_low1, False),
        mail(upp1, at_upp1, False),
    )

    @pl.when(even)
    def _():
        load(sep_lower, low, 0).start()
        load(sep_upper, upp, 1).start()
        load(sep_inv, inv, 2).start()

    @pl.when(odd)
    def _():
        load(sep_lower, low1, 0).start()
        load(sep_upper, upp1, 1).start()
        load(sep_inv, inv1, 2).start()

    @pl.when(top)
    def _():
        load(top_diag, diag, 3).start()

    load(int_lower, ilow, 5).start()
    load(int_upper, iupp, 6).start()
    load(int_inv, iinv, 7).start()

    barrier = pltpu.get_barrier_semaphore()
    reach = [sign * 2**power for power in range(levels) for sign in (1, -1)]
    for steps in reach:
        pl.semaphore_signal(barrier, inc=1, device_id={"tm": near(steps)}, device_id_type=MESH)
    pl.semaphore_wait(barrier, len(reach))

    def holds(height):
        return lax.rem(position, 2**height) == 0

    def coupled(height):
        return lax.rem(position // 2**height, 2) == 1

    def sends(height, act):
        offset = 2 ** (height - 1)
        mails = level_mail[height]
        if height == levels:
            diag_src, up_src = top_diag.at[0], top_coup.at[0]
        else:
            diag_src, up_src = diag, up

        def act_up():
            act(mails["c_up"], up_src, near(offset))

        def act_down():
            act(mails["c_down"], down, near(-offset))

        if height == levels:
            act_up()
        else:
            pl.when(coupled(height))(act_up)
            pl.when(coupled(height))(act_down)
        act(mails["a"], diag_src, near(offset))
        if height > 2:
            act(mails["b"], diag_src, near(-offset))

    def start(message, src, to):
        message.start(src, to)

    def finish(message, src, to):
        message.wait_send(src, to)

    parent = lax.rem(position, 4) == 2
    other = lax.rem(position, 4) == 0
    first_odd = lax.rem(position, 4) == 1
    last_odd = lax.rem(position, 4) == 3

    @pl.when(top)
    def _():
        odd_a.start(top_diag.at[0], near(1))
        sends(levels, start)

    @pl.when(odd)
    def _():
        back_low.start(sep_lower.at[0], near(-1))

    @pl.when(first_odd)
    def _():
        back_upp.start(sep_upper.at[0], near(-1))
        back_inv.start(sep_inv.at[0], near(-1))
        rail_b.relay(odd_a, near(-2))
        mirror(diag_a1)

    @pl.when(last_odd)
    def _():
        even_b.relay(rail_b, near(-1))
        back_upp.start(sep_upper.at[0], near(-1))
        back_inv.start(sep_inv.at[0], near(-1))
        mirror(diag_b1)

    @pl.when(even)
    def _():
        load(sep_lower, low, 0).wait()
        load(sep_upper, upp, 1).wait()
        load(sep_inv, inv, 2).wait()

    @pl.when(top)
    def _():
        load(top_diag, diag, 3).wait()

    for height in range(levels, 1, -1):
        offset = 2 ** (height - 1)
        mails = level_mail[height]
        if height < levels:
            pl.when(holds(height))(functools.partial(sends, height, start))

        @pl.when(lax.rem(position, 2**height) == offset)
        def _():
            mails["c_up"].wait_recv(me)
            if height == levels:
                flipped = coup[...].T
            else:
                from_below = jnp.where(coupled(height), 1.0, 0.0)
                value = coup[...].astype(jnp.float32)
                flipped = jnp.where(from_below > 0.5, value.T, value).astype(jnp.bfloat16)
            def upper_side():
                if height == 2:
                    even_b.wait_recv(me)
                else:
                    mails["b"].wait_recv(me)
                upper = diag_b1 if height == 2 else diag_b
                mirror(upper)
                toward_upper = product_transposed(low[...], flipped) + product(
                    upp[...], upper[...]
                )
                up[...] = toward_upper.astype(jnp.bfloat16)
                if height == 2:
                    coup1[...] = up[...].T
                    odd_c.start(coup1, near(1))

            mails["a"].wait_recv(me)
            mirror(diag_a)
            toward_lower = product(low[...], diag_a[...]) + product(upp[...], flipped)
            down[...] = toward_lower.astype(jnp.bfloat16)
            if height == 2:
                feed_c.start(down, near(-2))
            upper_side()
            diagonal = (
                inv[...].astype(jnp.float32)
                + product_transposed(down[...], low[...])
                + product_transposed(up[...], upp[...])
            )
            diag[...] = diagonal.astype(jnp.bfloat16)
            odd_a.start(diag, near(1))
            if height == 2:
                feed_b.start(diag, near(-2))

    late_b = lax.rem(position, 4) < 2
    late_a = lax.rem(position, 4) >= 2

    load(int_lower, ilow, 5).wait()
    load(int_upper, iupp, 6).wait()
    load(int_inv, iinv, 7).wait()

    def interior_own(own, coupling):
        value = (product(ilow[...], own[...]) + product(iupp[...], coupling)).astype(jnp.bfloat16)
        out_below[0] = value
        return product_transposed(value, ilow[...])

    def interior_next(coupling_product, following):
        value = (coupling_product + product(iupp[...], following[...])).astype(jnp.bfloat16)
        out_below[1] = value.T
        return product_transposed(value, iupp[...])

    def finish_interior(value):
        out_diag[1] = (part_int[...] + value).astype(jnp.bfloat16)

    @pl.when(even)
    def _():
        out_diag[0] = diag[...]
        diag_a1[...] = diag[...]

    @pl.when(odd)
    def _():
        load(sep_lower, low1, 0).wait()
        load(sep_upper, upp1, 1).wait()
        load(sep_inv, inv1, 2).wait()

    @pl.when(other)
    def _():
        odd_c.relay(feed_c, near(1))
        back_low.wait_recv(me)
        back_upp.wait_recv(me)
        back_inv.wait_recv(me)
        mirror(inv1)

    @pl.when(odd)
    def _():
        odd_c.wait_recv(me)

    @pl.when(late_b)
    def _():
        toward_lower = product(low1[...], diag_a1[...]) + product(upp1[...], coup1[...])
        down1[...] = toward_lower.astype(jnp.bfloat16)
        part_side[...] = product_transposed(low1[...], coup1[...])
        part_diag[...] = inv1[...].astype(jnp.float32) + product_transposed(down1[...], low1[...])

        @pl.when(even)
        def _():
            part_int[...] = iinv[...].astype(jnp.float32) + interior_own(diag_a1, down1[...])
            odd_b.relay(feed_b, near(1))

        @pl.when(odd)
        def _():
            odd_b.wait_recv(me)

        mirror(diag_b1)
        up1[...] = (part_side[...] + product(upp1[...], diag_b1[...])).astype(jnp.bfloat16)
        diagonal = part_diag[...] + product_transposed(up1[...], upp1[...])
        diag1[...] = diagonal.astype(jnp.bfloat16)

        @pl.when(even)
        def _():
            finish_interior(interior_next(product_transposed(ilow[...], down1[...]), diag1))

        @pl.when(odd)
        def _():
            out_diag[0] = diag1[...]
            part_int[...] = iinv[...].astype(jnp.float32) + interior_next(
                product(ilow[...], up1[...]), diag_b1
            )
            finish_interior(interior_own(diag1, up1[...].T))

    @pl.when(late_a)
    def _():
        @pl.when(even)
        def _():
            back_low.wait_recv(me)
            back_upp.wait_recv(me)

        toward_upper = product_transposed(low1[...], coup1[...]) + product(upp1[...], diag_b1[...])
        up1[...] = toward_upper.astype(jnp.bfloat16)
        part_side[...] = product(upp1[...], coup1[...])
        part_diag[...] = product_transposed(up1[...], upp1[...])

        @pl.when(odd)
        def _():
            part_diag[...] += inv1[...].astype(jnp.float32)
            part_int[...] = iinv[...].astype(jnp.float32) + interior_next(
                product(ilow[...], up1[...]), diag_b1
            )
            odd_a.wait_recv(me)
            mirror(diag_a1)

        toward_lower = product(low1[...], diag_a1[...]) + part_side[...]
        down1[...] = toward_lower.astype(jnp.bfloat16)
        part_diag[...] += product_transposed(down1[...], low1[...])

        @pl.when(even)
        def _():
            part_int[...] = iinv[...].astype(jnp.float32) + interior_own(diag_a1, down1[...])
            part_side[...] = product_transposed(ilow[...], down1[...])
            back_inv.wait_recv(me)
            mirror(inv1)
            diag1[...] = (part_diag[...] + inv1[...].astype(jnp.float32)).astype(jnp.bfloat16)
            finish_interior(interior_next(part_side[...], diag1))

        @pl.when(odd)
        def _():
            diag1[...] = part_diag[...].astype(jnp.bfloat16)
            out_diag[0] = diag1[...]
            finish_interior(interior_own(diag1, up1[...].T))

    for height in range(levels, 1, -1):
        pl.when(holds(height))(functools.partial(sends, height, finish))

    @pl.when(parent)
    def _():
        feed_c.wait_send(down, near(-2))
        feed_b.wait_send(diag, near(-2))

    @pl.when(even)
    def _():
        odd_a.wait_send(diag, near(1))
        odd_c.wait_send(coup1, near(1))

    @pl.when(other)
    def _():
        odd_b.wait_send(diag_b1, near(1))

    @pl.when(first_odd)
    def _():
        rail_b.wait_send(diag_a1, near(-2))

    @pl.when(last_odd)
    def _():
        even_b.wait_send(diag_b1, near(-1))

    @pl.when(odd)
    def _():
        back_low.wait_send(sep_lower.at[0], near(-1))
        back_upp.wait_send(sep_upper.at[0], near(-1))
        back_inv.wait_send(sep_inv.at[0], near(-1))


def hand_over(diag_from, below_from, diag_to, below_to, held, in_sem, out_sem):
    pairs = [
        (src.at[at], dst.at[at])
        for src, dst in ((diag_from, diag_to), (below_from, below_to))
        for at in range(2)
    ]
    ins = [
        pltpu.make_async_copy(src, held.at[at], in_sem.at[at]) for at, (src, _) in enumerate(pairs)
    ]
    outs = [
        pltpu.make_async_copy(held.at[at], dst, out_sem.at[at]) for at, (_, dst) in enumerate(pairs)
    ]
    for copy in ins:
        copy.start()
    for into, out in zip(ins, outs):
        into.wait()
        out.start()
    for copy in outs:
        copy.wait()


def solution(mesh):
    devices = mesh.shape["tm"]
    levels = min(4, devices // 4)

    def on_device(*blocks):
        size = blocks[0].shape[-1]
        sends, receives = semaphore_counts(levels, len(strips(size)))
        block = pltpu.VMEM((size, size), jnp.bfloat16)
        out = jax.ShapeDtypeStruct((2, size, size), jnp.bfloat16)
        found = pl.pallas_call(
            functools.partial(kernel, devices, levels),
            out_shape=(out, out),
            in_specs=[pl.BlockSpec(memory_space=pltpu.HBM)] * len(blocks),
            out_specs=[pl.BlockSpec(memory_space=pltpu.VMEM)] * 2,
            scratch_shapes=[block] * 21
            + [pltpu.VMEM((size, size), jnp.float32)] * 3
            + [
                pltpu.SemaphoreType.DMA((sends,)),
                pltpu.SemaphoreType.DMA((receives,)),
                pltpu.SemaphoreType.DMA((8,)),
            ],
            compiler_params=pltpu.CompilerParams(
                collective_id=0, has_side_effects=True, vmem_limit_bytes=63 * 2**20
            ),
            cost_estimate=pl.CostEstimate(
                flops=36 * size**3, bytes_accessed=24 * size**2, transcendentals=0
            ),
        )(*blocks)
        return pl.pallas_call(
            hand_over,
            out_shape=(out, out),
            in_specs=[pl.BlockSpec(memory_space=pl.ANY)] * 2,
            out_specs=[pl.BlockSpec(memory_space=pl.ANY)] * 2,
            scratch_shapes=[
                pltpu.VMEM((4, size, size), jnp.bfloat16),
                pltpu.SemaphoreType.DMA((4,)),
                pltpu.SemaphoreType.DMA((4,)),
            ],
            cost_estimate=pl.CostEstimate(
                flops=0, bytes_accessed=16 * size**2, transcendentals=0
            ),
        )(*found)

    spec = P(("rep", "tm"), None, None)
    return jax.shard_map(
        on_device, mesh=mesh, in_specs=(spec,) * 8, out_specs=(spec, spec), check_vma=False
    )
```
